768 devices in a mesh: blk: 192 (over z, x, y_lo, core), inner: 4 (over y_hi).
Axes of the slice: x: 4, y: 8 (y_hi: 4, y_lo: 2; y = y_hi * 2 + y_lo), z: 12, core: 2. Of those that a mesh axis runs over, the one named last changes fastest.
Arguments:
- clip_embed: float32 [196608, 512], P('blk'), may hold values from -30 to 30
- caption_embed: float32 [589824, 512], P(('blk', 'inner')), may hold values from -30 to 30
- caption_counts: int32 [196608], P('blk'), may hold values from 1 to 3, as said below
Outputs:
- clip_loss: float32 [196608], P('blk')
- caption_loss: float32 [589824], P(('blk', 'inner'))
The draws below stay inside these ranges and needn't reach their ends.
Inputs may be any that keep to these rules, and one draw needn't show every extreme that they name: `caption_counts`: the captions of the 256 clips of one device's aligned block total at most 768, and some block in every draw totals exactly 768.
All inputs are finite; a program needn't handle non-finite values.
Results may differ from the reference program's by a relative error of at most 0.0003.
Values sent between devices are 32-bit elements; how exact they have to be, the bound alone decides.
No kernel may reach another device: no remote copies, remote signals or barrier semaphores. Data moves between devices by JAX's collectives and lax.ppermute only.
A program may use at most 32 MiB of HBM per device.

```python
import jax
import jax.numpy as jnp
from jax import lax

E = 512
CLIP_SUB = 256
CLIP_GRP = 1024
CAP = 768
CLIPS = 196608
CAPS = 589824
N_BLK = 192
N_INNER = 4


def row_scales(key, rows):
    return jnp.exp(jax.random.uniform(key, (rows, 1), jnp.float32, jnp.log(0.3), jnp.log(3.0)))


def draw_clip_embed(key, part):
    key = jax.random.fold_in(key, 5)
    key_scale, key_vals = jax.random.split(key, 2)
    scales = row_scales(key_scale, CLIPS)
    return jax.random.truncated_normal(key_vals, -4.0, 4.0, (CLIPS, E), jnp.float32) * scales


def draw_caption_embed(key, part):
    key = jax.random.fold_in(key, 7)
    key_scale, key_vals = jax.random.split(key, 2)
    scales = row_scales(key_scale, CAPS)
    return jax.random.truncated_normal(key_vals, -4.0, 4.0, (CAPS, E), jnp.float32) * scales


def draw_caption_counts(key, part):
    key = jax.random.fold_in(key, 9)
    key_heavy, key_pick, key_extra = jax.random.split(key, 3)
    device_count = CLIPS // CLIP_SUB
    heavy = (jax.random.randint(key_heavy, (device_count,), 0, 32) == 0) | (jnp.arange(device_count) == jax.random.randint(key_pick, (), 0, device_count))
    extra = (jax.random.randint(key_extra, (CLIPS,), 0, 8) == 0).astype(jnp.int32)
    return jnp.where(heavy[jnp.arange(CLIPS) // CLIP_SUB], 3, 1 + extra).astype(jnp.int32)


def setup_inputs(seed: int = 0) -> dict:
    key_list = jax.random.split(jax.random.key(seed), 4)
    return {
        "clip_embed": draw_clip_embed(jax.random.fold_in(key_list[3], 71), 0),
        "caption_embed": draw_caption_embed(jax.random.fold_in(key_list[3], 71), 0),
        "caption_counts": draw_caption_counts(jax.random.fold_in(key_list[3], 71), 0),
    }


def reference(clip_embed, caption_embed, caption_counts):
    clips = clip_embed.reshape(N_BLK, CLIP_GRP, E)
    captions = caption_embed.reshape(N_BLK, N_INNER, CAP, E)
    counts = caption_counts.reshape(N_BLK, N_INNER, CLIP_SUB)
    ends = jnp.cumsum(counts, axis=2).astype(jnp.int32)
    starts = ends - counts
    lengths = ends[:, :, -1]
    slots = jnp.arange(CAP, dtype=jnp.int32)
    live_all = slots[None, None, :] < lengths[:, :, None]
    same_block = jnp.arange(N_INNER)[:, None, None, None] == jnp.arange(N_INNER)[None, None, :, None]
    factor = 1.0 / (E ** 0.5)

    def visit_group(col_acc, group):
        indices = [(group + shift_by) % N_BLK for shift_by in range(-2, 3)]
        window = jnp.stack([captions[index] for index in indices]).reshape(-1, E)
        live = jnp.stack([live_all[index] for index in indices]).reshape(-1)
        scores = jnp.einsum("ce,je->cj", clips[group], window, precision=lax.Precision.HIGHEST) * factor
        masked = jnp.where(live[None, :], scores, -1e30)
        row_max = jnp.max(masked, axis=1)
        row_lse = row_max + jnp.log(jnp.sum(jnp.exp(masked - row_max[:, None]), axis=1))
        col_max = jnp.max(scores, axis=0)
        col_lse = (col_max + jnp.log(jnp.sum(jnp.exp(scores - col_max[None, :]), axis=0))).reshape(5, N_INNER, CAP)
        for number, index in enumerate(indices):
            col_acc = col_acc.at[index].set(jnp.logaddexp(col_acc[index], col_lse[number]))
        own_scores = scores.reshape(CLIP_GRP, 5, N_INNER * CAP)[:, 2]
        owned = same_block & (starts[group][:, :, None, None] <= slots[None, None, None, :]) & (slots[None, None, None, :] < ends[group][:, :, None, None])
        owned = owned.reshape(CLIP_GRP, N_INNER * CAP).astype(jnp.float32)
        pos_clip = jnp.sum(owned * own_scores, axis=1)
        pos_cap = jnp.sum(owned * own_scores, axis=0)
        clip_loss = row_lse - pos_clip / counts[group].reshape(-1).astype(jnp.float32)
        return col_acc, (clip_loss, pos_cap)

    start_acc = jnp.full((N_BLK, N_INNER, CAP), -jnp.inf, jnp.float32)
    col_acc, (clip_loss, pos_cap) = lax.scan(visit_group, start_acc, jnp.arange(N_BLK, dtype=jnp.int32))
    caption_loss = jnp.where(live_all, col_acc - pos_cap.reshape(N_BLK, N_INNER, CAP), 0.0)
    return clip_loss.reshape(-1), caption_loss.reshape(-1)
```

```python
import math

import jax
import jax.numpy as jnp
from jax import lax
from jax.experimental import pallas as pl
from jax.experimental.pallas import tpu as pltpu
from jax.sharding import PartitionSpec as P

AXES = ("blk", "inner")
LN2 = math.log(2.0)
DEAD = -1e30
LANES = 128
TILE = 256
NT = (((1,), (1,)), ((), ()))


def exchange_pairs(chips, inner):
    def place(chip, core, k):
        return ((chip % chips) * 2 + core) * inner + k % inner

    def after(chip, core, k):
        return place(chip + 1, core, k if chip % 2 == 0 else k + 1)

    def before(chip, core, k):
        return place(chip - 1, core, k if chip % 2 == 1 else k - 1)

    everyone = [(c, s, k) for c in range(chips) for s in range(2) for k in range(inner)]
    near = [(place(*d), (before if d[1] == 0 else after)(*d)) for d in everyone]
    far = [(place(*d), (after if d[1] == 0 else before)(*d)) for d in everyone]
    swap = [(place(c, s, k), place(c, 1 - s, k)) for c, s, k in everyone]
    around = [[(place(c, s, k), place(c, s, k + n)) for c, s, k in everyone] for n in range(1, inner)]
    return near, far, swap, around


def back(pairs):
    return [(target, source) for source, target in pairs]


def send(value, pairs):
    return lax.ppermute(value, AXES, pairs)


def lse2(a, b):
    top = jnp.maximum(a, b)
    return top + jnp.log2(jnp.exp2(a - top) + jnp.exp2(b - top))


def split(x):
    high = x.astype(jnp.bfloat16)
    low = (x - high.astype(jnp.float32)).astype(jnp.bfloat16)
    return high, low


def load_captions(ref, rows, out):
    depth = ref.shape[1]
    for at in range(0, rows, TILE):
        high, low = split(ref[at : at + TILE, :])
        out[at : at + TILE, 0:depth] = high
        out[at : at + TILE, depth : 2 * depth] = low
        out[at : at + TILE, 2 * depth : 3 * depth] = high


def to_lanes(column):
    eye = lax.broadcasted_iota(jnp.int32, (LANES, LANES), 0) == lax.broadcasted_iota(jnp.int32, (LANES, LANES), 1)
    parts = []
    for at in range(0, column.shape[0], LANES):
        parts.append(jnp.sum(jnp.where(eye, column[at : at + LANES], 0.0), axis=0, keepdims=True))
    return jnp.concatenate(parts, axis=1)


def scores_of(clips, at, captions, scale):
    high, low = split(clips[at : at + TILE, :] * scale)
    lhs = jnp.concatenate([high, high, low], axis=1)
    return lax.dot_general(lhs, captions[...], NT, preferred_element_type=jnp.float32)


def visit(clips, captions, bias, scale, row_refs, cols, scores_seen=None):
    top, total = cols
    for at in range(0, clips.shape[0], TILE):
        scores = scores_of(clips, at, captions, scale)
        if scores_seen is not None:
            scores_seen(at, scores)
        masked = scores + bias
        row_max = jnp.max(masked, axis=1, keepdims=True)
        row_sum = jnp.sum(jnp.exp2(masked - row_max), axis=1, keepdims=True)
        lanes = to_lanes(row_max + jnp.log2(row_sum))
        row_refs(at, lanes)
        tile_max = jnp.max(scores, axis=0, keepdims=True)
        new_top = tile_max if top is None else jnp.maximum(top, tile_max)
        tile_sum = jnp.sum(jnp.exp2(scores - new_top), axis=0, keepdims=True)
        total = tile_sum if top is None else total * jnp.exp2(top - new_top) + tile_sum
        top = new_top
    return top, total


def slot_bias(length, slots):
    return jnp.where(lax.broadcasted_iota(jnp.int32, (1, slots), 1) < length, 0.0, DEAD)


def own_kernel(scale, place, own, other, captions, counts, rows, rows_other, cols, pos, pos_cap, packed):
    slots = captions.shape[0]
    counted = counts[...]
    sub = counted.shape[1]
    ahead = lax.broadcasted_iota(jnp.int32, (sub, sub), 1)
    here = lax.broadcasted_iota(jnp.int32, (sub, sub), 0)
    starts = jnp.sum(jnp.where(ahead < here, counted, 0.0), axis=1, keepdims=True)
    ends = jnp.sum(jnp.where(ahead <= here, counted, 0.0), axis=1, keepdims=True)
    bias = slot_bias(place[1], slots)
    mine = place[0]
    load_captions(captions, slots, packed)
    slot = lax.broadcasted_iota(jnp.int32, (sub, slots), 1).astype(jnp.float32)
    pos_cap[...] = jnp.zeros_like(pos_cap)

    def seen(at, scores):
        @pl.when(mine == at // sub)
        def _():
            owned = jnp.where((starts <= slot) & (slot < ends), scores, 0.0)
            pos[:, at : at + TILE] = to_lanes(jnp.sum(owned, axis=1, keepdims=True))
            pos_cap[...] = jnp.sum(owned, axis=0, keepdims=True)

        @pl.when(mine != at // sub)
        def _():
            pos[:, at : at + TILE] = jnp.zeros((1, TILE), jnp.float32)

    def keep(at, lanes):
        rows[:, at : at + TILE] = lanes

    def keep_other(at, lanes):
        rows_other[:, at : at + TILE] = lanes

    state = visit(own, packed, bias, scale, keep, (None, None), seen)
    top, total = visit(other, packed, bias, scale, keep_other, state)
    cols[...] = top + jnp.log2(total)


def near_kernel(scale, own, other, arrived, rows_in, rows_other_in, rows, rows_other, cols, packed):
    slots = cols.shape[1]
    bias = slot_bias(arrived[slots : slots + 1, 0:1].astype(jnp.int32), slots)
    load_captions(arrived, slots, packed)

    def keep(at, lanes):
        rows[:, at : at + TILE] = lse2(rows_in[:, at : at + TILE], lanes)

    def keep_other(at, lanes):
        rows_other[:, at : at + TILE] = lse2(rows_other_in[:, at : at + TILE], lanes)

    state = visit(other, packed, bias, scale, keep_other, (None, None))
    top, total = visit(own, packed, bias, scale, keep, state)
    cols[...] = top + jnp.log2(total)


def far_kernel(scale, own, arrived, rows_in, rows_sent, pos, packet, cols, packed):
    slots = cols.shape[1]
    bias = slot_bias(arrived[slots : slots + 1, 0:1].astype(jnp.int32), slots)
    load_captions(arrived, slots, packed)

    def keep(at, lanes):
        before = lse2(rows_in[:, at : at + TILE], rows_sent[:, at : at + TILE])
        packet[:, at : at + TILE] = lse2(before, lanes)

    top, total = visit(own, packed, bias, scale, keep, (None, None))
    cols[...] = top + jnp.log2(total)
    packet[:, own.shape[0] :] = pos[...]


def last_kernel(place, mine, first, second, third, counts, cols, near, far, pos_cap, clip_loss, caption_loss):
    rows = counts.shape[1]
    parts = [ref[:, :rows] for ref in (mine, first, second, third)]
    top = jnp.maximum(jnp.maximum(parts[0], parts[1]), jnp.maximum(parts[2], parts[3]))
    total = sum(jnp.exp2(part - top) for part in parts)
    pos = sum(ref[:, rows:] for ref in (mine, first, second, third))
    clip_loss[...] = LN2 * (top + jnp.log2(total) - pos / counts[...].astype(jnp.float32))
    parts = [cols[...], near[...], far[...]]
    top = jnp.maximum(jnp.maximum(parts[0], parts[1]), parts[2])
    total = sum(jnp.exp2(part - top) for part in parts)
    loss = LN2 * (top + jnp.log2(total) - pos_cap[...])
    slot = lax.broadcasted_iota(jnp.int32, loss.shape, 1)
    caption_loss[...] = jnp.where(slot < place[1], loss, 0.0)


def call(kernel, out_widths, operands, scratch=(), scalars=False, flops=0):
    whole = pl.BlockSpec(memory_space=pltpu.VMEM)
    first = [pl.BlockSpec(memory_space=pltpu.SMEM)] if scalars else []
    return pl.pallas_call(
        kernel,
        out_shape=[jax.ShapeDtypeStruct((1, width), jnp.float32) for width in out_widths],
        in_specs=first + [whole] * (len(operands) - len(first)),
        out_specs=[whole] * len(out_widths),
        scratch_shapes=list(scratch),
        compiler_params=pltpu.CompilerParams(vmem_limit_bytes=48 * 1024 * 1024),
        cost_estimate=pl.CostEstimate(flops=flops, bytes_accessed=4 * 1024 * 1024, transcendentals=flops // 1024),
    )(*operands)


def solution(mesh):
    inner = mesh.shape["inner"]
    near, far, swap, around = exchange_pairs(mesh.shape["blk"] // 2, inner)

    def shards(clip_embed, caption_embed, caption_counts):
        rows, depth = clip_embed.shape
        slots = caption_embed.shape[0]
        scale = math.log2(math.e) / math.sqrt(depth)
        inner_index = lax.axis_index("inner")
        counts = lax.dynamic_index_in_dim(caption_counts.reshape(inner, rows // inner), inner_index, 0, True)
        length = jnp.sum(counts)
        place = jnp.stack([inner_index.astype(jnp.int32), length])
        block = jnp.concatenate([caption_embed, jnp.full((8, depth), length.astype(jnp.float32))], axis=0)
        near_block = send(block, near)
        far_block = send(block, far)
        other = send(clip_embed, swap)
        packed = pltpu.VMEM((slots, 3 * depth), jnp.bfloat16)
        work = 6 * rows * slots * depth

        def bound(kernel):
            def run(*refs):
                kernel(scale, *refs)

            return run

        rows_own, rows_other, cols, pos, pos_cap = call(
            bound(own_kernel),
            (rows, rows, slots, rows, slots),
            (place, clip_embed, other, caption_embed, counts.astype(jnp.float32)),
            [packed],
            True,
            2 * work,
        )
        rows_own, rows_other, near_cols = call(
            bound(near_kernel),
            (rows, rows, slots),
            (clip_embed, other, near_block, rows_own, rows_other),
            [packed],
            False,
            2 * work,
        )
        near_cols = send(near_cols, back(near))
        rows_sent = send(rows_other, swap)
        packet, far_cols = call(
            bound(far_kernel),
            (2 * rows, slots),
            (clip_embed, far_block, rows_own, rows_sent, pos),
            [packed],
            False,
            work,
        )
        far_cols = send(far_cols, back(far))
        packets = [send(packet, pairs) for pairs in around]
        clip_loss, caption_loss = call(
            last_kernel,
            (rows, slots),
            (place, packet, *packets, caption_counts.reshape(1, rows), cols, near_cols, far_cols, pos_cap),
            (),
            True,
        )
        return clip_loss.reshape(rows), caption_loss.reshape(slots)

    in_specs = (P("blk", None), P(AXES, None), P("blk"))
    out_specs = (P("blk"), P(AXES))
    return jax.shard_map(shards, mesh=mesh, in_specs=in_specs, out_specs=out_specs, check_vma=False)
```

```python
import functools
import math

import jax
import jax.numpy as jnp
from jax import lax
from jax.experimental import pallas as pl
from jax.experimental.pallas import tpu as pltpu
from jax.sharding import PartitionSpec as P

AXES = ("blk", "inner")
LN2 = math.log(2.0)
DEAD = -1e30
LANES = 128
TILE = 256
NT = (((1,), (1,)), ((), ()))


def exchange_pairs(chips, inner):
    def place(chip, core, k):
        return ((chip % chips) * 2 + core) * inner + k % inner

    def after(chip, core, k):
        return place(chip + 1, core, k if chip % 2 == 0 else k + 1)

    def before(chip, core, k):
        return place(chip - 1, core, k if chip % 2 == 1 else k - 1)

    everyone = [(c, s, k) for c in range(chips) for s in range(2) for k in range(inner)]
    near = [(place(*d), (before if d[1] == 0 else after)(*d)) for d in everyone]
    far = [(place(*d), (after if d[1] == 0 else before)(*d)) for d in everyone]
    swap = [(place(c, s, k), place(c, 1 - s, k)) for c, s, k in everyone]
    around = [[(place(c, s, k), place(c, s, k ^ n)) for c, s, k in everyone] for n in (1, inner - 1)]
    return near, far, swap, around


def back(pairs):
    return [(target, source) for source, target in pairs]


def send(value, pairs):
    return lax.ppermute(value, AXES, pairs)


def lse2(a, b):
    top = jnp.maximum(a, b)
    return top + jnp.log2(jnp.exp2(a - top) + jnp.exp2(b - top))


def split(x):
    high = x.astype(jnp.bfloat16)
    low = (x - high.astype(jnp.float32)).astype(jnp.bfloat16)
    return high, low


def load_captions(ref, rows, out):
    depth = ref.shape[1]
    for at in range(0, rows, TILE):
        high, low = split(ref[at : at + TILE, :])
        out[at : at + TILE, 0:depth] = high
        out[at : at + TILE, depth : 2 * depth] = low
        out[at : at + TILE, 2 * depth : 3 * depth] = high


def to_lanes(column):
    eye = lax.broadcasted_iota(jnp.int32, (LANES, LANES), 0) == lax.broadcasted_iota(jnp.int32, (LANES, LANES), 1)
    parts = []
    for at in range(0, column.shape[0], LANES):
        parts.append(jnp.sum(jnp.where(eye, column[at : at + LANES], 0.0), axis=0, keepdims=True))
    return jnp.concatenate(parts, axis=1)


def product(clips, captions, scale):
    high, low = split(clips * scale)
    lhs = jnp.concatenate([high, high, low], axis=1)
    return lax.dot_general(lhs, captions[...], NT, preferred_element_type=jnp.float32)


def visit(clips, captions, bias, scale, keep, cols):
    top, total = cols
    tiles = [ref[at : at + TILE, :] for ref in clips for at in range(0, ref.shape[0], TILE)]
    for number, tile in enumerate(tiles):
        at = number * TILE
        scores = product(tile, captions, scale)
        masked = scores + bias
        row_max = jnp.max(masked, axis=1, keepdims=True)
        row_sum = jnp.sum(jnp.exp2(masked - row_max), axis=1, keepdims=True)
        keep(at, to_lanes(row_max + jnp.log2(row_sum)))
        tile_max = jnp.max(scores, axis=0, keepdims=True)
        new_top = tile_max if top is None else jnp.maximum(top, tile_max)
        tile_sum = jnp.sum(jnp.exp2(scores - new_top), axis=0, keepdims=True)
        total = tile_sum if top is None else total * jnp.exp2(top - new_top) + tile_sum
        top = new_top
    return top, total


def slot_bias(length, slots):
    return jnp.where(lax.broadcasted_iota(jnp.int32, (1, slots), 1) < length, 0.0, DEAD)


def own_counts(counts, mine):
    lines = counts.shape[0] // lax.axis_size("inner")
    here = counts[pl.ds(mine * lines, lines), :]
    return jnp.concatenate([here[n : n + 1] for n in range(lines)], axis=1)


def live_length(block, slots):
    return block[slots : slots + 1, 0:1].astype(jnp.int32)


def block_kernel(captions, counts, block, length):
    slots = captions.shape[0]
    block[0:slots, :] = captions[...]
    total = jnp.sum(own_counts(counts, lax.axis_index("inner")).astype(jnp.float32), axis=1, keepdims=True)
    block[slots:, :] = jnp.broadcast_to(total, (block.shape[0] - slots, block.shape[1]))
    length[...] = jnp.broadcast_to(total, length.shape)


def own_kernel(scale, own, block, counts, rows, cols, pos, pos_cap, packed):
    slots = packed.shape[0]
    mine = lax.axis_index("inner")
    counted = own_counts(counts, mine).astype(jnp.float32)
    sub = counted.shape[1]
    ahead = lax.broadcasted_iota(jnp.int32, (sub, sub), 1)
    here = lax.broadcasted_iota(jnp.int32, (sub, sub), 0)
    starts = jnp.sum(jnp.where(ahead < here, counted, 0.0), axis=1, keepdims=True)
    ends = jnp.sum(jnp.where(ahead <= here, counted, 0.0), axis=1, keepdims=True)
    bias = slot_bias(live_length(block, slots), slots)
    load_captions(block, slots, packed)

    def keep(at, lanes):
        rows[:, at : at + TILE] = lanes

    top, total = visit((own,), packed, bias, scale, keep, (None, None))
    cols[...] = top + jnp.log2(total)
    first = pl.multiple_of(mine * sub, sub)
    scores = product(own[pl.ds(first, sub), :], packed, scale)
    slot = lax.broadcasted_iota(jnp.int32, (sub, slots), 1).astype(jnp.float32)
    owned = jnp.where((starts <= slot) & (slot < ends), scores, 0.0)
    pos[...] = jnp.zeros_like(pos)
    pos[:, pl.ds(first, sub)] = to_lanes(jnp.sum(owned, axis=1, keepdims=True))
    pos_cap[...] = jnp.sum(owned, axis=0, keepdims=True)


def partner_kernel(scale, other, other_rest, block, cols_in, rows_other, cols, packed):
    slots = packed.shape[0]
    bias = slot_bias(live_length(block, slots), slots)
    load_captions(block, slots, packed)

    def keep_other(at, lanes):
        rows_other[:, at : at + TILE] = lanes

    top, total = visit((other, other_rest), packed, bias, scale, keep_other, (None, None))
    cols[...] = lse2(cols_in[...], top + jnp.log2(total))


def near_kernel(scale, own, other, other_rest, arrived, length, rows_in, rows_other_in, rows, rows_other, cols, packed):
    slots = cols.shape[1]
    bias = slot_bias(live_length(length, 0), slots)
    load_captions(arrived, slots, packed)

    def keep(at, lanes):
        rows[:, at : at + TILE] = lse2(rows_in[:, at : at + TILE], lanes)

    def keep_other(at, lanes):
        rows_other[:, at : at + TILE] = lse2(rows_other_in[:, at : at + TILE], lanes)

    state = visit((other, other_rest), packed, bias, scale, keep_other, (None, None))
    top, total = visit((own,), packed, bias, scale, keep, state)
    cols[...] = jnp.broadcast_to(top + jnp.log2(total), cols.shape)


def far_kernel(scale, own, arrived, rows_in, rows_sent, pos, packet, cols, packed):
    slots = cols.shape[1]
    bias = slot_bias(live_length(arrived, slots), slots)
    load_captions(arrived, slots, packed)

    def keep(at, lanes):
        before = lse2(rows_in[:, at : at + TILE], rows_sent[:, at : at + TILE])
        packet[:, at : at + TILE] = lse2(before, lanes)

    top, total = visit((own,), packed, bias, scale, keep, (None, None))
    cols[...] = jnp.broadcast_to(top + jnp.log2(total), cols.shape)
    packet[:, own.shape[0] :] = pos[...]


def merge_kernel(mine, sent, merged):
    rows = mine.shape[1] // 2
    merged[:, :rows] = lse2(mine[:, :rows], sent[:, :rows])
    merged[:, rows:] = mine[:, rows:] + sent[:, rows:]


def last_kernel(mine, sent, counts, length, cols, near, far, pos_cap, clip_loss, caption_loss):
    rows = counts.shape[1]
    slots = cols.shape[1]
    pos = mine[:, rows:] + sent[:, rows:]
    total = lse2(mine[:, :rows], sent[:, :rows])
    clip_loss[...] = LN2 * (total - pos / counts[...].astype(jnp.float32))
    parts = [cols[...], near[0:1, :], far[0:1, :]]
    top = jnp.maximum(jnp.maximum(parts[0], parts[1]), parts[2])
    total = sum(jnp.exp2(part - top) for part in parts)
    loss = LN2 * (top + jnp.log2(total) - pos_cap[...])
    slot = lax.broadcasted_iota(jnp.int32, loss.shape, 1)
    live = slot < live_length(length, 0)
    caption_loss[...] = jnp.where(live, loss, 0.0).reshape(caption_loss.shape)


def call(kernel, out_shapes, operands, scratch=(), flops=0):
    whole = pl.BlockSpec(memory_space=pltpu.VMEM)
    return pl.pallas_call(
        kernel,
        out_shape=[jax.ShapeDtypeStruct(shape, jnp.float32) for shape in out_shapes],
        in_specs=[whole] * len(operands),
        out_specs=[whole] * len(out_shapes),
        scratch_shapes=list(scratch),
        compiler_params=pltpu.CompilerParams(vmem_limit_bytes=24 * 1024 * 1024),
        cost_estimate=pl.CostEstimate(flops=flops, bytes_accessed=4 * 1024 * 1024, transcendentals=flops // 1024),
    )(*operands)


def solution(mesh):
    inner = mesh.shape["inner"]
    near, far, swap, around = exchange_pairs(mesh.shape["blk"] // 2, inner)

    def shards(clip_embed, caption_embed, caption_counts):
        rows, depth = clip_embed.shape
        slots = caption_embed.shape[0]
        scale = math.log2(math.e) / math.sqrt(depth)
        packed = [pltpu.VMEM((slots, 3 * depth), jnp.bfloat16)]
        work = 6 * rows * slots * depth
        row, col = (1, rows), (1, slots)

        def scaled(kernel):
            return functools.partial(kernel, scale)

        counts = caption_counts.reshape(rows // LANES, LANES)
        near_block = send(caption_embed, near)
        other = [send(half, swap) for half in jnp.split(clip_embed, 2)]
        block, length = call(block_kernel, [(slots + 8, depth), (1, LANES)], (caption_embed, counts))
        rows_own, cols, pos, pos_cap = call(
            scaled(own_kernel), [row, col, row, col], (clip_embed, block, counts), packed, work
        )
        sent_block, sent_length, rows_own = lax.optimization_barrier((block, length, rows_own))
        far_block = send(sent_block, far)
        near_length = send(sent_length, near)
        rows_other, cols = call(scaled(partner_kernel), [row, col], (*other, block, cols), packed, work)
        rows_own, rows_other, near_cols = call(
            scaled(near_kernel), [row, row, (16, slots)], (clip_embed, *other, near_block, near_length, rows_own, rows_other), packed, 2 * work
        )
        rows_sent = send(rows_other, swap)
        packet, far_cols = call(
            scaled(far_kernel), [(1, 2 * rows), (8, slots)], (clip_embed, far_block, rows_own, rows_sent, pos), packed, work
        )
        far_cols = send(far_cols, back(far))
        near_cols = send(near_cols, back(near))
        sent = send(packet, around[0])
        (packet,) = call(merge_kernel, [(1, 2 * rows)], (packet, sent))
        sent = send(packet, around[1])
        clip_loss, caption_loss = call(
            last_kernel,
            [row, (slots,)],
            (packet, sent, caption_counts.reshape(row), length, cols, near_cols, far_cols, pos_cap),
        )
        return clip_loss.reshape(rows), caption_loss

    in_specs = (P("blk", None), P(AXES, None), P("blk"))
    out_specs = (P("blk"), P(AXES))
    return jax.shard_map(shards, mesh=mesh, in_specs=in_specs, out_specs=out_specs, check_vma=False)
```

```python
import functools
import math

import jax
import jax.numpy as jnp
from jax import lax
from jax.experimental import pallas as pl
from jax.experimental.pallas import tpu as pltpu
from jax.sharding import PartitionSpec as P

AXES = ("blk", "inner")
LN2 = math.log(2.0)
DEAD = -1e30
LANES = 128
TILE = 256
NT = (((1,), (1,)), ((), ()))


def exchange_pairs(chips, inner):
    def place(chip, core, k):
        return ((chip % chips) * 2 + core) * inner + k % inner

    def after(chip, core, k):
        return place(chip + 1, core, k if chip % 2 == 0 else k + 1)

    def before(chip, core, k):
        return place(chip - 1, core, k if chip % 2 == 1 else k - 1)

    everyone = [(c, s, k) for c in range(chips) for s in range(2) for k in range(inner)]
    near = [(place(*d), (before if d[1] == 0 else after)(*d)) for d in everyone]
    far = [(place(*d), (after if d[1] == 0 else before)(*d)) for d in everyone]
    swap = [(place(c, s, k), place(c, 1 - s, k)) for c, s, k in everyone]
    around = [[(place(c, s, k), place(c, s, k ^ n)) for c, s, k in everyone] for n in (1, inner - 1)]
    return near, far, swap, around


def back(pairs):
    return [(target, source) for source, target in pairs]


def send(value, pairs):
    return lax.ppermute(value, AXES, pairs)


def lse2(a, b):
    top = jnp.maximum(a, b)
    return top + jnp.log2(jnp.exp2(a - top) + jnp.exp2(b - top))


def split(x):
    high = x.astype(jnp.bfloat16)
    low = (x - high.astype(jnp.float32)).astype(jnp.bfloat16)
    return high, low


def load_captions(ref, rows, out):
    depth = ref.shape[1]
    for at in range(0, rows, TILE):
        high, low = split(ref[at : at + TILE, :])
        out[at : at + TILE, 0:depth] = high
        out[at : at + TILE, depth : 2 * depth] = low
        out[at : at + TILE, 2 * depth : 3 * depth] = high


def to_lanes(column):
    eye = lax.broadcasted_iota(jnp.int32, (LANES, LANES), 0) == lax.broadcasted_iota(jnp.int32, (LANES, LANES), 1)
    parts = []
    for at in range(0, column.shape[0], LANES):
        parts.append(jnp.sum(jnp.where(eye, column[at : at + LANES], 0.0), axis=0, keepdims=True))
    return jnp.concatenate(parts, axis=1)


def product(clips, captions, scale):
    high, low = split(clips * scale)
    lhs = jnp.concatenate([high, high, low], axis=1)
    return lax.dot_general(lhs, captions[...], NT, preferred_element_type=jnp.float32)


def visit(clips, captions, bias, scale, keep, cols):
    top, total = cols
    tiles = [ref[at : at + TILE, :] for ref in clips for at in range(0, ref.shape[0], TILE)]
    for number, tile in enumerate(tiles):
        at = number * TILE
        scores = product(tile, captions, scale)
        masked = scores + bias
        row_max = jnp.max(masked, axis=1, keepdims=True)
        row_sum = jnp.sum(jnp.exp2(masked - row_max), axis=1, keepdims=True)
        keep(at, to_lanes(row_max + jnp.log2(row_sum)))
        tile_max = jnp.max(scores, axis=0, keepdims=True)
        new_top = tile_max if top is None else jnp.maximum(top, tile_max)
        tile_sum = jnp.sum(jnp.exp2(scores - new_top), axis=0, keepdims=True)
        total = tile_sum if top is None else total * jnp.exp2(top - new_top) + tile_sum
        top = new_top
    return top, total


def slot_bias(length, slots):
    return jnp.where(lax.broadcasted_iota(jnp.int32, (1, slots), 1) < length, 0.0, DEAD)


def own_counts(counts, mine):
    lines = counts.shape[0] // lax.axis_size("inner")
    here = counts[pl.ds(mine * lines, lines), :]
    return jnp.concatenate([here[n : n + 1] for n in range(lines)], axis=1)


def live_length(block, slots):
    return block[slots : slots + 1, 0:1].astype(jnp.int32)


def block_kernel(captions, counts, block, length):
    slots = captions.shape[0]
    block[0:slots, :] = captions[...]
    total = jnp.sum(own_counts(counts, lax.axis_index("inner")).astype(jnp.float32), axis=1, keepdims=True)
    block[slots:, :] = jnp.broadcast_to(total, (block.shape[0] - slots, block.shape[1]))
    length[...] = jnp.broadcast_to(total, length.shape)


def own_kernel(scale, own, block, counts, rows, cols, pos, pos_cap, packed):
    slots = packed.shape[0]
    mine = lax.axis_index("inner")
    counted = own_counts(counts, mine).astype(jnp.float32)
    sub = counted.shape[1]
    ahead = lax.broadcasted_iota(jnp.int32, (sub, sub), 1)
    here = lax.broadcasted_iota(jnp.int32, (sub, sub), 0)
    starts = jnp.sum(jnp.where(ahead < here, counted, 0.0), axis=1, keepdims=True)
    ends = jnp.sum(jnp.where(ahead <= here, counted, 0.0), axis=1, keepdims=True)
    bias = slot_bias(live_length(block, slots), slots)
    load_captions(block, slots, packed)

    def keep(at, lanes):
        rows[:, at : at + TILE] = lanes

    top, total = visit((own,), packed, bias, scale, keep, (None, None))
    cols[...] = top + jnp.log2(total)
    first = pl.multiple_of(mine * sub, sub)
    scores = product(own[pl.ds(first, sub), :], packed, scale)
    slot = lax.broadcasted_iota(jnp.int32, (sub, slots), 1).astype(jnp.float32)
    owned = jnp.where((starts <= slot) & (slot < ends), scores, 0.0)
    pos[...] = jnp.zeros_like(pos)
    pos[:, pl.ds(first, sub)] = to_lanes(jnp.sum(owned, axis=1, keepdims=True))
    pos_cap[...] = jnp.sum(owned, axis=0, keepdims=True)


def partner_kernel(scale, other, other_rest, block, cols_in, rows_other, cols, packed):
    slots = packed.shape[0]
    bias = slot_bias(live_length(block, slots), slots)
    load_captions(block, slots, packed)

    def keep_other(at, lanes):
        rows_other[:, at : at + TILE] = lanes

    top, total = visit((other, other_rest), packed, bias, scale, keep_other, (None, None))
    cols[...] = lse2(cols_in[...], top + jnp.log2(total))


def near_kernel(scale, own, other, other_rest, arrived, length, rows_in, rows_other_in, rows, rows_other, cols, packed):
    slots = cols.shape[1]
    bias = slot_bias(live_length(length, 0), slots)
    load_captions(arrived, slots, packed)

    def keep(at, lanes):
        rows[:, at : at + TILE] = lse2(rows_in[:, at : at + TILE], lanes)

    def keep_other(at, lanes):
        rows_other[:, at : at + TILE] = lse2(rows_other_in[:, at : at + TILE], lanes)

    state = visit((other, other_rest), packed, bias, scale, keep_other, (None, None))
    top, total = visit((own,), packed, bias, scale, keep, state)
    cols[...] = jnp.broadcast_to(top + jnp.log2(total), cols.shape)


def far_kernel(scale, own, arrived, rows_in, rows_sent, pos, packet, cols, packed):
    slots = cols.shape[1]
    bias = slot_bias(live_length(arrived, slots), slots)
    load_captions(arrived, slots, packed)

    def keep(at, lanes):
        before = lse2(rows_in[:, at : at + TILE], rows_sent[:, at : at + TILE])
        packet[:, at : at + TILE] = lse2(before, lanes)

    top, total = visit((own,), packed, bias, scale, keep, (None, None))
    cols[...] = jnp.broadcast_to(top + jnp.log2(total), cols.shape)
    packet[:, own.shape[0] :] = pos[...]


def merge_kernel(mine, sent, merged):
    rows = mine.shape[1] // 2
    merged[:, :rows] = lse2(mine[:, :rows], sent[:, :rows])
    merged[:, rows:] = mine[:, rows:] + sent[:, rows:]


def last_kernel(mine, sent, counts, length, cols, near, far, pos_cap, clip_loss, caption_loss):
    rows = counts.shape[1]
    slots = cols.shape[1]
    pos = mine[:, rows:] + sent[:, rows:]
    total = lse2(mine[:, :rows], sent[:, :rows])
    clip_loss[...] = LN2 * (total - pos / counts[...].astype(jnp.float32))
    parts = [cols[...], near[0:1, :], far[0:1, :]]
    top = jnp.maximum(jnp.maximum(parts[0], parts[1]), parts[2])
    total = sum(jnp.exp2(part - top) for part in parts)
    loss = LN2 * (top + jnp.log2(total) - pos_cap[...])
    slot = lax.broadcasted_iota(jnp.int32, loss.shape, 1)
    live = slot < live_length(length, 0)
    caption_loss[...] = jnp.where(live, loss, 0.0).reshape(caption_loss.shape)


def call(kernel, out_shapes, operands, scratch=(), flops=0):
    whole = pl.BlockSpec(memory_space=pltpu.VMEM)
    return pl.pallas_call(
        kernel,
        out_shape=[jax.ShapeDtypeStruct(shape, jnp.float32) for shape in out_shapes],
        in_specs=[whole] * len(operands),
        out_specs=[whole] * len(out_shapes),
        scratch_shapes=list(scratch),
        compiler_params=pltpu.CompilerParams(vmem_limit_bytes=24 * 1024 * 1024),
        cost_estimate=pl.CostEstimate(flops=flops, bytes_accessed=4 * 1024 * 1024, transcendentals=flops // 1024),
    )(*operands)


def solution(mesh):
    inner = mesh.shape["inner"]
    near, far, swap, around = exchange_pairs(mesh.shape["blk"] // 2, inner)

    def shards(clip_embed, caption_embed, caption_counts):
        rows, depth = clip_embed.shape
        slots = caption_embed.shape[0]
        scale = math.log2(math.e) / math.sqrt(depth)
        packed = [pltpu.VMEM((slots, 3 * depth), jnp.bfloat16)]
        work = 6 * rows * slots * depth
        row, col = (1, rows), (1, slots)

        def scaled(kernel):
            return functools.partial(kernel, scale)

        counts = caption_counts.reshape(rows // LANES, LANES)
        near_block = send(caption_embed, near)
        other = [send(half, swap) for half in jnp.split(clip_embed, 2)]
        block, length = call(block_kernel, [(slots + 8, depth), (1, LANES)], (caption_embed, counts))
        rows_own, cols, pos, pos_cap = call(
            scaled(own_kernel), [row, col, row, col], (clip_embed, block, counts), packed, work
        )
        sent_block, sent_length, rows_own = lax.optimization_barrier((block, length, rows_own))
        far_block = send(sent_block, far)
        near_length = send(sent_length, near)
        rows_other, cols = call(scaled(partner_kernel), [row, col], (*other, block, cols), packed, work)
        rows_own, rows_other, near_cols = call(
            scaled(near_kernel), [row, row, (16, slots)], (clip_embed, *other, near_block, near_length, rows_own, rows_other), packed, 2 * work
        )
        rows_sent = send(rows_other, swap)
        packet, far_cols = call(
            scaled(far_kernel), [(1, 2 * rows), (4, slots)], (clip_embed, far_block, rows_own, rows_sent, pos), packed, work
        )
        far_cols = send(far_cols, back(far))
        near_cols = send(near_cols, back(near))
        sent = send(packet, around[0])
        (packet,) = call(merge_kernel, [(1, 2 * rows)], (packet, sent))
        sent = send(packet, around[1])
        clip_loss, caption_loss = call(
            last_kernel,
            [row, (slots,)],
            (packet, sent, caption_counts.reshape(row), length, cols, near_cols, far_cols, pos_cap),
        )
        return clip_loss.reshape(rows), caption_loss

    in_specs = (P("blk", None), P(AXES, None), P("blk"))
    out_specs = (P("blk"), P(AXES))
    return jax.shard_map(shards, mesh=mesh, in_specs=in_specs, out_specs=out_specs, check_vma=False)
```

```python
import functools
import math

import jax
import jax.numpy as jnp
from jax import lax
from jax.experimental import pallas as pl
from jax.experimental.pallas import tpu as pltpu
from jax.sharding import PartitionSpec as P

AXES = ("blk", "inner")
LN2 = math.log(2.0)
DEAD = -1e30
LANES = 128
TILE = 256
FULL = 512
NT = (((1,), (1,)), ((), ()))


def exchange_pairs(chips, inner):
    def place(chip, core, k):
        return ((chip % chips) * 2 + core) * inner + k % inner

    def after(chip, core, k):
        return place(chip + 1, core, k if chip % 2 == 0 else k + 1)

    def before(chip, core, k):
        return place(chip - 1, core, k if chip % 2 == 1 else k - 1)

    everyone = [(c, s, k) for c in range(chips) for s in range(2) for k in range(inner)]
    near = [(place(*d), (before if d[1] == 0 else after)(*d)) for d in everyone]
    far = [(place(*d), (after if d[1] == 0 else before)(*d)) for d in everyone]
    swap = [(place(c, s, k), place(c, 1 - s, k)) for c, s, k in everyone]
    around = [[(place(c, s, k), place(c, s, k ^ n)) for c, s, k in everyone] for n in (1, inner - 1)]
    return near, far, swap, around


def back(pairs):
    return [(target, source) for source, target in pairs]


def send(value, pairs):
    return lax.ppermute(value, AXES, pairs)


def lse2(a, b):
    top = jnp.maximum(a, b)
    return top + jnp.log2(jnp.exp2(a - top) + jnp.exp2(b - top))


def split(x):
    high = x.astype(jnp.bfloat16)
    low = (x - high.astype(jnp.float32)).astype(jnp.bfloat16)
    return high, low


def load_captions(ref, first, last, out):
    depth = ref.shape[1]
    for at in range(first, last, TILE):
        high, low = split(ref[at : at + TILE, :])
        out[at : at + TILE, 0:depth] = high
        out[at : at + TILE, depth : 2 * depth] = low
        out[at : at + TILE, 2 * depth : 3 * depth] = high


def to_lanes(column):
    eye = lax.broadcasted_iota(jnp.int32, (LANES, LANES), 0) == lax.broadcasted_iota(jnp.int32, (LANES, LANES), 1)
    parts = []
    for at in range(0, column.shape[0], LANES):
        parts.append(jnp.sum(jnp.where(eye, column[at : at + LANES], 0.0), axis=0, keepdims=True))
    return jnp.concatenate(parts, axis=1)


def product(clips, captions, scale):
    high, low = split(clips * scale)
    lhs = jnp.concatenate([high, high, low], axis=1)
    return lax.dot_general(lhs, captions, NT, preferred_element_type=jnp.float32)


def visit(groups, source, length, packed, scale, keep_cols):
    slots = packed.shape[0]
    bias = jnp.where(lax.broadcasted_iota(jnp.int32, (1, slots), 1) < length, 0.0, DEAD)

    def part(first, last):
        load_captions(source, first, last, packed)
        captions = packed[first:last, :]
        top = total = None
        for clips, keep in groups:
            tiles = [ref[at : at + TILE, :] for ref in clips for at in range(0, ref.shape[0], TILE)]
            for number, tile in enumerate(tiles):
                scores = product(tile, captions, scale)
                masked = scores + bias[:, first:last]
                row_max = jnp.max(masked, axis=1, keepdims=True)
                row_sum = jnp.sum(jnp.exp2(masked - row_max), axis=1, keepdims=True)
                keep(number * TILE, to_lanes(row_max + jnp.log2(row_sum)), first > 0)
                tile_max = jnp.max(scores, axis=0, keepdims=True)
                new_top = tile_max if top is None else jnp.maximum(top, tile_max)
                tile_sum = jnp.sum(jnp.exp2(scores - new_top), axis=0, keepdims=True)
                total = tile_sum if top is None else total * jnp.exp2(top - new_top) + tile_sum
                top = new_top
        keep_cols(first, last, top + jnp.log2(total))

    full = min(FULL, slots)
    part(0, full)
    if full < slots:
        keep_cols(full, slots, jnp.zeros((1, slots - full), jnp.float32))

        @pl.when(length > full)
        def _():
            part(full, slots)


def own_counts(counts, mine):
    lines = counts.shape[0] // lax.axis_size("inner")
    here = counts[pl.ds(mine * lines, lines), :]
    return jnp.concatenate([here[n : n + 1] for n in range(lines)], axis=1)


def live_length(block, slots):
    return jnp.max(block[slots : slots + 1, 0:LANES]).astype(jnp.int32)


def block_kernel(captions, counts, block, length):
    slots = captions.shape[0]
    block[0:slots, :] = captions[...]
    total = jnp.sum(own_counts(counts, lax.axis_index("inner")).astype(jnp.float32), axis=1, keepdims=True)
    block[slots:, :] = jnp.broadcast_to(total, (block.shape[0] - slots, block.shape[1]))
    length[...] = jnp.broadcast_to(total, length.shape)


def own_kernel(scale, own, block, counts, rows, cols, pos, pos_cap, packed):
    slots = packed.shape[0]
    mine = lax.axis_index("inner")
    counted = own_counts(counts, mine).astype(jnp.float32)
    sub = counted.shape[1]
    ahead = lax.broadcasted_iota(jnp.int32, (sub, sub), 1)
    here = lax.broadcasted_iota(jnp.int32, (sub, sub), 0)
    starts = jnp.sum(jnp.where(ahead < here, counted, 0.0), axis=1, keepdims=True)
    ends = jnp.sum(jnp.where(ahead <= here, counted, 0.0), axis=1, keepdims=True)

    def keep(at, lanes, again):
        rows[:, at : at + TILE] = lse2(rows[:, at : at + TILE], lanes) if again else lanes

    def keep_cols(first, last, values):
        cols[:, first:last] = values

    visit([((own,), keep)], block, live_length(block, slots), packed, scale, keep_cols)
    load_captions(block, min(FULL, slots), slots, packed)
    first = pl.multiple_of(mine * sub, sub)
    scores = product(own[pl.ds(first, sub), :], packed[...], scale)
    slot = lax.broadcasted_iota(jnp.int32, (sub, slots), 1).astype(jnp.float32)
    owned = jnp.where((starts <= slot) & (slot < ends), scores, 0.0)
    pos[...] = jnp.zeros_like(pos)
    pos[:, pl.ds(first, sub)] = to_lanes(jnp.sum(owned, axis=1, keepdims=True))
    pos_cap[...] = jnp.sum(owned, axis=0, keepdims=True)


def partner_kernel(scale, other, other_rest, block, cols_in, rows_other, cols, packed):
    slots = packed.shape[0]

    def keep(at, lanes, again):
        rows_other[:, at : at + TILE] = lse2(rows_other[:, at : at + TILE], lanes) if again else lanes

    def keep_cols(first, last, values):
        cols[:, first:last] = lse2(cols_in[:, first:last], values)

    visit([((other, other_rest), keep)], block, live_length(block, slots), packed, scale, keep_cols)


def near_kernel(scale, own, other, other_rest, arrived, length, rows_in, rows_other_in, rows, rows_other, cols, packed):
    def keep(at, lanes, again):
        before = rows if again else rows_in
        rows[:, at : at + TILE] = lse2(before[:, at : at + TILE], lanes)

    def keep_other(at, lanes, again):
        before = rows_other if again else rows_other_in
        rows_other[:, at : at + TILE] = lse2(before[:, at : at + TILE], lanes)

    def keep_cols(first, last, values):
        cols[:, first:last] = jnp.broadcast_to(values, (cols.shape[0], last - first))

    groups = [((other, other_rest), keep_other), ((own,), keep)]
    visit(groups, arrived, live_length(length, 0), packed, scale, keep_cols)


def far_kernel(scale, own, arrived, rows_in, rows_sent, pos, packet, cols, packed):
    def keep(at, lanes, again):
        if again:
            before = packet[:, at : at + TILE]
        else:
            before = lse2(rows_in[:, at : at + TILE], rows_sent[:, at : at + TILE])
        packet[:, at : at + TILE] = lse2(before, lanes)

    def keep_cols(first, last, values):
        cols[:, first:last] = jnp.broadcast_to(values, (cols.shape[0], last - first))

    visit([((own,), keep)], arrived, live_length(arrived, packed.shape[0]), packed, scale, keep_cols)
    packet[:, own.shape[0] :] = pos[...]


def merge_kernel(mine, sent, merged):
    rows = mine.shape[1] // 2
    merged[:, :rows] = lse2(mine[:, :rows], sent[:, :rows])
    merged[:, rows:] = mine[:, rows:] + sent[:, rows:]


def last_kernel(mine, sent, counts, length, cols, near, far, pos_cap, clip_loss, caption_loss):
    rows = counts.shape[1]
    slots = cols.shape[1]
    pos = mine[:, rows:] + sent[:, rows:]
    total = lse2(mine[:, :rows], sent[:, :rows])
    clip_loss[...] = LN2 * (total - pos / counts[...].astype(jnp.float32))
    parts = [cols[...], near[0:1, :], far[0:1, :]]
    top = jnp.maximum(jnp.maximum(parts[0], parts[1]), parts[2])
    total = sum(jnp.exp2(part - top) for part in parts)
    loss = LN2 * (top + jnp.log2(total) - pos_cap[...])
    slot = lax.broadcasted_iota(jnp.int32, loss.shape, 1)
    live = slot < live_length(length, 0)
    caption_loss[...] = jnp.where(live, loss, 0.0).reshape(caption_loss.shape)


def call(kernel, out_shapes, operands, scratch=(), flops=0):
    whole = pl.BlockSpec(memory_space=pltpu.VMEM)
    return pl.pallas_call(
        kernel,
        out_shape=[jax.ShapeDtypeStruct(shape, jnp.float32) for shape in out_shapes],
        in_specs=[whole] * len(operands),
        out_specs=[whole] * len(out_shapes),
        scratch_shapes=list(scratch),
        compiler_params=pltpu.CompilerParams(vmem_limit_bytes=24 * 1024 * 1024),
        cost_estimate=pl.CostEstimate(flops=flops, bytes_accessed=4 * 1024 * 1024, transcendentals=flops // 1024),
    )(*operands)


def solution(mesh):
    inner = mesh.shape["inner"]
    near, far, swap, around = exchange_pairs(mesh.shape["blk"] // 2, inner)

    def shards(clip_embed, caption_embed, caption_counts):
        rows, depth = clip_embed.shape
        slots = caption_embed.shape[0]
        scale = math.log2(math.e) / math.sqrt(depth)
        packed = [pltpu.VMEM((slots, 3 * depth), jnp.bfloat16)]
        work = 6 * rows * slots * depth
        row, col = (1, rows), (1, slots)

        def scaled(kernel):
            return functools.partial(kernel, scale)

        counts = caption_counts.reshape(rows // LANES, LANES)
        near_block = send(caption_embed, near)
        other = [send(half, swap) for half in jnp.split(clip_embed, 2)]
        block, length = call(block_kernel, [(slots + 8, depth), (1, LANES)], (caption_embed, counts))
        rows_own, cols, pos, pos_cap = call(
            scaled(own_kernel), [row, col, row, col], (clip_embed, block, counts), packed, work
        )
        sent_block, sent_length, rows_own = lax.optimization_barrier((block, length, rows_own))
        far_block = send(sent_block, far)
        near_length = send(sent_length, near)
        rows_other, cols = call(scaled(partner_kernel), [row, col], (*other, block, cols), packed, work)
        rows_own, rows_other, near_cols = call(
            scaled(near_kernel), [row, row, (16, slots)], (clip_embed, *other, near_block, near_length, rows_own, rows_other), packed, 2 * work
        )
        rows_sent = send(rows_other, swap)
        packet, far_cols = call(
            scaled(far_kernel), [(1, 2 * rows), (4, slots)], (clip_embed, far_block, rows_own, rows_sent, pos), packed, work
        )
        far_cols = send(far_cols, back(far))
        near_cols = send(near_cols, back(near))
        sent = send(packet, around[0])
        (packet,) = call(merge_kernel, [(1, 2 * rows)], (packet, sent))
        sent = send(packet, around[1])
        clip_loss, caption_loss = call(
            last_kernel,
            [row, (slots,)],
            (packet, sent, caption_counts.reshape(row), length, cols, near_cols, far_cols, pos_cap),
        )
        return clip_loss.reshape(rows), caption_loss

    in_specs = (P("blk", None), P(AXES, None), P("blk"))
    out_specs = (P("blk"), P(AXES))
    return jax.shard_map(shards, mesh=mesh, in_specs=in_specs, out_specs=out_specs, check_vma=False)
```
